32 devices in a mesh: node: 4 (over x, core), dev: 8 (over z, y).
Axes of the slice: x: 2, y: 2, z: 4, core: 2. Of those that a mesh axis runs over, the one named last changes fastest.
Arguments:
- tokens: bfloat16 [8192, 7168], P(('node', 'dev')), may hold values from -6 to 6
- grad_out: bfloat16 [8192, 7168], P(('node', 'dev')), may hold values from -1.796875 to 1.796875
- router_gates: bfloat16 [8192, 8], P(('node', 'dev')), may hold values from 0.049804688 to 1
- expert_ids: int32 [8192, 8], P(('node', 'dev')), may hold values from 0 to 255, as said below
- slot_plan: int32 [256, 2], replicated, may hold values from 0 to 8, as said below
- w_gate: bfloat16 [4, 7168, 2048], P(None, 'dev', 'node'), may hold values from -0.0625 to 0.0625
- w_up: bfloat16 [4, 7168, 2048], P(None, 'dev', 'node'), may hold values from -0.0625 to 0.0625
- w_down: bfloat16 [4, 2048, 7168], P(None, 'node', 'dev'), may hold values from -0.125 to 0.125
Outputs:
- grad_tokens: bfloat16 [8192, 7168], P(('node', 'dev'))
- grad_gates: float32 [8192, 8], P(('node', 'dev'))
- grad_w_gate: bfloat16 [4, 7168, 2048], P(None, 'dev', 'node')
- grad_w_up: bfloat16 [4, 7168, 2048], P(None, 'dev', 'node')
- grad_w_down: bfloat16 [4, 2048, 7168], P(None, 'node', 'dev')
The draws below stay inside these ranges and needn't reach their ends.
Inputs may be any that keep to these rules, and one draw needn't show every extreme that they name: `expert_ids`: each token names 8 different experts. Within one block of 256 tokens (the tokens of one device), at most 4 pairs name any one expert that has slots, and in every draw one expert that has slots is named exactly 2 * 2 times in every block. `slot_plan`: exactly 4 rows hold slots: each such row holds two different slots, and every slot 0 .. 7 stands in exactly one row. Every entry of the other rows equals 8.
All inputs are finite; a program needn't handle non-finite values.
Results may differ from the reference program's by a relative error of at most 0.0059.
Values may be sent and summed in bfloat16 or wider, within the bound.
A program may use at most 128 MiB of HBM per device.

```python
import jax
import jax.numpy as jnp
from jax import lax

D = 7168
F = 2048
EXPERTS = 256
TOP = 8
REPS = 2
TOK_DEV = 256
CAP = 2
SLOTS = 8
ROUND = 4
TOKENS = 8192


def routing_tables(key):
    sub_keys = [jax.random.fold_in(key, 7001 + number) for number in range(8)]
    block_count = TOKENS // TOK_DEV
    expert_order = jax.random.permutation(sub_keys[0], EXPERTS).astype(jnp.int32)
    round_ids = expert_order[:ROUND]
    slot_order = jax.random.permutation(sub_keys[1], SLOTS).astype(jnp.int32).reshape(ROUND, REPS)
    slot_plan = jnp.full((EXPERTS, REPS), SLOTS, jnp.int32).at[round_ids].set(slot_order)
    full_expert = jax.random.randint(sub_keys[2], (), 0, ROUND)
    picks = jax.random.randint(sub_keys[3], (block_count, ROUND), 0, 2 * CAP + 1)
    picks = jnp.where(jnp.arange(ROUND)[None, :] == full_expert, 2 * CAP, picks)
    scores = jax.random.randint(sub_keys[4], (block_count, ROUND, TOK_DEV), 0, 1 << 20) * TOK_DEV + jnp.arange(TOK_DEV, dtype=jnp.int32)
    standing = jnp.argsort(jnp.argsort(scores, axis=-1), axis=-1)
    chosen = (standing < picks[:, :, None]).transpose(0, 2, 1).reshape(TOKENS, ROUND)
    placing = jnp.cumsum(chosen.astype(jnp.int32), axis=1) - 1
    taken = jnp.sum(chosen.astype(jnp.int32), axis=1)
    column = jnp.arange(TOP, dtype=jnp.int32)
    landing = chosen[:, None, :] & (placing[:, None, :] == column[None, :, None])
    round_pick = jnp.sum(jnp.where(landing, round_ids[None, None, :], 0), axis=-1)
    others = EXPERTS - ROUND
    offset = jax.random.randint(sub_keys[5], (TOKENS, 1), 0, others)
    filler = expert_order[ROUND + (offset + column[None, :] - taken[:, None]) % others]
    picked = jnp.where(column[None, :] < taken[:, None], round_pick, filler)
    shuffle = jax.random.randint(sub_keys[6], (TOKENS, TOP), 0, 1 << 20) * TOP + column[None, :]
    column_order = jnp.argsort(shuffle, axis=1)
    expert_ids = jnp.take_along_axis(picked, column_order, axis=1).astype(jnp.int32)
    return (expert_ids, slot_plan)


def draw_expert_ids(key, part):
    return routing_tables(key)[0]


def draw_slot_plan(key, part):
    return routing_tables(key)[1]


def steps_of(stream_key, dims, cuts, least, high):
    factor_of = 1.0
    for axis_at, blocks in cuts:
        steps = jax.random.uniform(jax.random.fold_in(jax.random.fold_in(stream_key, 6), axis_at), (blocks,), jnp.float32, least / len(cuts), high / len(cuts))
        factor_of = factor_of * jnp.repeat(jnp.exp(steps), dims[axis_at] // blocks).reshape((-1,) + (1,) * (len(dims) - 1 - axis_at))
    return factor_of


def noise(key, shape, scale, limit, pieces=(), held_as=jnp.bfloat16):
    values = scale * jax.random.normal(key, shape, jnp.float32)
    if pieces:
        values = values * steps_of(key, shape, pieces, -0.22, 0.18)
    return jnp.clip(values, -limit, limit).astype(held_as)


def setup_inputs(seed: int = 0) -> dict:
    streams_of = jax.random.split(jax.random.key(seed), 9)
    return {
        "tokens": noise(streams_of[0], (TOKENS, D), 1.0, 6.0, ((0, 32),)),
        "grad_out": noise(streams_of[1], (TOKENS, D), 0.3, 1.796875, ((0, 32),)),
        "router_gates": jnp.clip(0.049804688 + 0.9501953 * jax.random.uniform(streams_of[2], (TOKENS, TOP), jnp.float32) ** steps_of(streams_of[2], (TOKENS, TOP), ((0, 32),), -0.2, 0.2), 0.049804688, 1.0).astype(jnp.bfloat16),
        "expert_ids": draw_expert_ids(jax.random.fold_in(streams_of[8], 71), 0),
        "slot_plan": draw_slot_plan(jax.random.fold_in(streams_of[8], 71), 0),
        "w_gate": noise(streams_of[5], (ROUND, D, F), D ** -0.5, 0.0625, ((1, 8), (2, 4))),
        "w_up": noise(streams_of[6], (ROUND, D, F), D ** -0.5, 0.0625, ((1, 8), (2, 4))),
        "w_down": noise(streams_of[7], (ROUND, F, D), F ** -0.5, 0.125, ((1, 4), (2, 8))),
    }


def served_pairs(expert_ids, slot_plan):
    block_count = TOKENS // TOK_DEV
    first_slot = slot_plan[:, 0][expert_ids].astype(jnp.int32)
    second_slot = slot_plan[:, 1][expert_ids].astype(jnp.int32)
    is_live = first_slot < SLOTS
    first_hot = (first_slot.reshape(block_count, TOK_DEV * TOP, 1) == jnp.arange(SLOTS, dtype=jnp.int32)).astype(jnp.int32)
    running = (jnp.cumsum(first_hot, axis=1) - 1).astype(jnp.int32)
    pair_order = jnp.sum(first_hot * running, axis=-1).astype(jnp.int32).reshape(TOKENS, TOP)
    pair_slot = jnp.where(pair_order % 2 == 0, first_slot, second_slot).astype(jnp.int32)
    block_index = (jnp.arange(TOKENS, dtype=jnp.int32) // TOK_DEV)[:, None]
    row_index = (block_index * CAP + pair_order // 2).astype(jnp.int32)
    return is_live, pair_slot, row_index


def reference(tokens, grad_out, router_gates, expert_ids, slot_plan, w_gate, w_up, w_down):
    is_live, pair_slot, row_index = served_pairs(expert_ids, slot_plan)
    row_total = (TOKENS // TOK_DEV) * CAP
    token_index = jnp.broadcast_to(jnp.arange(TOKENS, dtype=jnp.int32)[:, None], (TOKENS, TOP))
    pair_index = jnp.arange(TOKENS * TOP, dtype=jnp.int32).reshape(TOKENS, TOP)
    slot_key = jnp.where(is_live, pair_slot, SLOTS).astype(jnp.int32)
    row_token = jnp.full((SLOTS, row_total), -1, jnp.int32).at[slot_key, row_index].set(token_index, mode="drop")
    row_pair = jnp.full((SLOTS, row_total), -1, jnp.int32).at[slot_key, row_index].set(pair_index, mode="drop")
    in_round = (slot_plan[:, 0] < SLOTS).astype(jnp.int32)
    expert_rank = (jnp.cumsum(in_round) - 1).astype(jnp.int32)
    holder = jnp.any(slot_plan[:, :, None] == jnp.arange(SLOTS, dtype=jnp.int32), axis=1)
    slot_rank = jnp.sum(jnp.where(holder, expert_rank[:, None], 0), axis=0).astype(jnp.int32)
    rank_match = (in_round[:, None] > 0) & (expert_rank[:, None] == jnp.arange(ROUND, dtype=jnp.int32)[None, :])
    slot_pairs = jnp.sum(jnp.where(rank_match[:, :, None], slot_plan[:, None, :], 0), axis=0).astype(jnp.int32)
    flat_gates = router_gates.reshape(TOKENS * TOP)

    def one_slot(slot_id):
        live_token = row_token[slot_id]
        live_pair = row_pair[slot_id]
        present = live_token >= 0
        safe_token = jnp.maximum(live_token, 0)
        safe_pair = jnp.maximum(live_pair, 0)
        rows_x = jnp.where(present[:, None], tokens[safe_token], jnp.zeros((), tokens.dtype))
        rows_dy = jnp.where(present[:, None], grad_out[safe_token], jnp.zeros((), grad_out.dtype))
        rows_gate = jnp.where(present, flat_gates[safe_pair].astype(jnp.float32), jnp.zeros((), jnp.float32))
        expert_pos = slot_rank[slot_id]
        gate_w = w_gate[expert_pos]
        up_w = w_up[expert_pos]
        down_w = w_down[expert_pos]
        gate_pre = jnp.dot(rows_x, gate_w, preferred_element_type=jnp.float32)
        up_pre = jnp.dot(rows_x, up_w, preferred_element_type=jnp.float32)
        back_proj = jnp.dot(rows_dy, down_w.T, preferred_element_type=jnp.float32)
        sigmoid_gate = jax.nn.sigmoid(gate_pre)
        active = gate_pre * sigmoid_gate
        hidden = active * up_pre
        scaled_back = rows_gate[:, None] * back_proj
        d_gate = (scaled_back * up_pre * sigmoid_gate * (1.0 + gate_pre * (1.0 - sigmoid_gate))).astype(jnp.bfloat16)
        d_up = (scaled_back * active).astype(jnp.bfloat16)
        scaled_hidden = (rows_gate[:, None] * hidden).astype(jnp.bfloat16)
        gate_terms = jnp.sum(back_proj * hidden, axis=-1)
        grad_rows = jnp.dot(d_gate, gate_w.T, preferred_element_type=jnp.float32) + jnp.dot(d_up, up_w.T, preferred_element_type=jnp.float32)
        slot_gate = jnp.dot(rows_x.T, d_gate, preferred_element_type=jnp.float32).astype(jnp.bfloat16)
        slot_up = jnp.dot(rows_x.T, d_up, preferred_element_type=jnp.float32).astype(jnp.bfloat16)
        slot_down = jnp.dot(scaled_hidden.T, rows_dy, preferred_element_type=jnp.float32).astype(jnp.bfloat16)
        return slot_gate, slot_up, slot_down, grad_rows, gate_terms

    slot_gate, slot_up, slot_down, grad_rows, gate_terms = lax.map(one_slot, jnp.arange(SLOTS, dtype=jnp.int32))

    def pair_sum(slot_stack):
        left = slot_stack[slot_pairs[:, 0]].astype(jnp.float32)
        right = slot_stack[slot_pairs[:, 1]].astype(jnp.float32)
        return (left + right).astype(jnp.bfloat16)

    grad_w_gate = pair_sum(slot_gate)
    grad_w_up = pair_sum(slot_up)
    grad_w_down = pair_sum(slot_down)
    token_key = jnp.where(row_token >= 0, row_token, TOKENS).reshape(-1)
    pair_key = jnp.where(row_pair >= 0, row_pair, TOKENS * TOP).reshape(-1)
    grad_tokens = jnp.zeros((TOKENS, D), jnp.float32).at[token_key].add(grad_rows.reshape(-1, D), mode="drop").astype(jnp.bfloat16)
    grad_gates = jnp.zeros((TOKENS * TOP,), jnp.float32).at[pair_key].add(gate_terms.reshape(-1), mode="drop").reshape(TOKENS, TOP)
    return grad_tokens, grad_gates, grad_w_gate, grad_w_up, grad_w_down
```

```python
import jax
import jax.numpy as jnp
from jax import lax
from jax.sharding import PartitionSpec as P

REPS = 2
CAP = 2
PER = REPS * CAP
F32 = jnp.float32
BF16 = jnp.bfloat16


def choose(expert_ids, router_gates, slot_plan, slots, experts):
    tok = expert_ids.shape[0]
    total = slot_plan.shape[0]
    live = slot_plan[:, 0] < slots
    ids = jnp.arange(total, dtype=jnp.int32)
    rank = jnp.sum(jnp.where((ids[None, :] < ids[:, None]) & live[None, :], 1, 0), axis=1)
    hot = jnp.sum(
        jnp.where(live[None, :] & (rank[None, :] == jnp.arange(experts)[:, None]), ids[None, :], 0),
        axis=1,
    )
    match = expert_ids[None, :, :] == hot[:, None, None]
    named = jnp.any(match, axis=2)
    gate = jnp.sum(jnp.where(match, router_gates.astype(F32)[None], 0.0), axis=2)
    t = jnp.arange(tok)
    before = (t[:, None] < t[None, :]).astype(BF16)
    order = jnp.dot(named.astype(BF16), before, preferred_element_type=F32)
    pick = named[:, None, :] & (order[:, None, :] == jnp.arange(PER, dtype=F32)[None, :, None])
    row_gate = jnp.sum(jnp.where(pick, gate[:, None, :], 0.0), axis=2)
    return pick.reshape(experts * PER, tok).astype(BF16), row_gate.reshape(-1), match


def local(tokens, grad_out, router_gates, expert_ids, slot_plan, w_gate, w_up, w_down):
    nd = lax.axis_size("dev")
    nn = lax.axis_size("node")
    tok, width = tokens.shape
    experts, cols, hid = w_gate.shape
    rows = experts * PER
    pick, row_gate, match = choose(expert_ids, router_gates, slot_plan, nd, experts)
    x_rows = jnp.dot(pick, tokens, preferred_element_type=F32).astype(BF16)
    dy_rows = jnp.dot(pick, grad_out, preferred_element_type=F32).astype(BF16)
    x_rows = x_rows.reshape(rows, nd, cols).transpose(1, 0, 2)
    dy_rows = dy_rows.reshape(rows, nd, cols).transpose(1, 0, 2)
    gate_line = jnp.zeros((1, cols), BF16).at[0, :rows].set(row_gate.astype(BF16))
    gate_line = jnp.broadcast_to(gate_line[None], (nd, 1, cols))
    sent = jnp.concatenate([x_rows, dy_rows, gate_line], axis=1)
    got = lax.all_to_all(sent, "dev", split_axis=0, concat_axis=0, tiled=True)
    got = lax.all_gather(got, "node", axis=0, tiled=False)
    per_expert = nn * nd * PER
    xs = got[:, :, :rows].reshape(nn, nd, experts, PER, cols).transpose(2, 0, 1, 3, 4)
    xs = xs.reshape(experts, per_expert, cols)
    dys = got[:, :, rows : 2 * rows].reshape(nn, nd, experts, PER, cols).transpose(2, 0, 1, 3, 4)
    dys = dys.reshape(experts, per_expert, cols)
    gates = got[:, :, 2 * rows, :rows].reshape(nn, nd, experts, PER).transpose(2, 0, 1, 3)
    part = experts * per_expert // nd
    gates = gates.reshape(nd, part)
    me = lax.axis_index("dev")
    node = lax.axis_index("node")
    my_gate = jnp.sum(
        jnp.where(jnp.arange(nd)[:, None] == me, gates.astype(F32), 0.0), axis=0
    )[:, None]

    def widen(a, b, spec):
        r = jnp.einsum(spec, a, b, preferred_element_type=F32).astype(BF16)
        return r.reshape(nd, part, hid)

    pre = jnp.stack(
        [
            widen(xs, w_gate, "jrd,jdh->jrh"),
            widen(xs, w_up, "jrd,jdh->jrh"),
            widen(dys, w_down, "jrd,jhd->jrh"),
        ],
        axis=1,
    )
    pre = lax.all_to_all(pre, "dev", split_axis=0, concat_axis=0, tiled=True)
    sums = jnp.sum(pre.astype(F32), axis=0)
    gate_pre, up_pre, back = sums[0], sums[1], sums[2]
    sig = jax.nn.sigmoid(gate_pre)
    act = gate_pre * sig
    hidden = act * up_pre
    scaled = my_gate * back
    d_gate = (scaled * up_pre * sig * (1.0 + gate_pre * (1.0 - sig))).astype(BF16)
    d_up = (scaled * act).astype(BF16)
    s_hid = (my_gate * hidden).astype(BF16)
    gate_terms = jnp.sum(back * hidden, axis=-1)
    full = lax.all_gather(jnp.stack([d_gate, d_up, s_hid]), "dev", axis=1, tiled=False)
    full = full.reshape(3, experts, per_expert, hid)
    spread = jnp.where(jnp.arange(nd)[:, None] == me, gate_terms[None, :], 0.0)
    spread = lax.psum(spread.reshape(experts, nn, nd, PER), ("node", "dev"))
    dg, du, sh = full[0], full[1], full[2]
    row_grad = jnp.einsum("jrh,jdh->jrd", dg, w_gate, preferred_element_type=F32)
    row_grad = row_grad + jnp.einsum("jrh,jdh->jrd", du, w_up, preferred_element_type=F32)
    row_grad = row_grad.reshape(experts, nn, nd, PER, cols).transpose(1, 2, 0, 3, 4)
    row_grad = lax.psum_scatter(row_grad, "node", scatter_dimension=0, tiled=False)
    back_rows = lax.all_to_all(row_grad, "dev", split_axis=0, concat_axis=0, tiled=True)
    back_rows = back_rows.reshape(nd, rows, cols).transpose(1, 0, 2).reshape(rows, width)
    high = back_rows.astype(BF16)
    low = (back_rows - high.astype(F32)).astype(BF16)
    grad_tokens = jnp.einsum(
        "qt,qd->td",
        jnp.concatenate([pick, pick], axis=0),
        jnp.concatenate([high, low], axis=0),
        preferred_element_type=F32,
    ).astype(BF16)
    mine = lax.dynamic_slice(spread, (0, node, me, 0), (experts, 1, 1, PER)).reshape(experts, PER, 1)
    pair_val = jnp.sum(jnp.where(pick.reshape(experts, PER, tok) > 0, mine, 0.0), axis=1)
    grad_gates = jnp.sum(jnp.where(match, pair_val[:, :, None], 0.0), axis=0)
    grad_w_gate = jnp.einsum("jrd,jrh->jdh", xs, dg, preferred_element_type=F32).astype(BF16)
    grad_w_up = jnp.einsum("jrd,jrh->jdh", xs, du, preferred_element_type=F32).astype(BF16)
    grad_w_down = jnp.einsum("jrh,jrd->jhd", sh, dys, preferred_element_type=F32).astype(BF16)
    return (grad_tokens, grad_gates, grad_w_gate, grad_w_up, grad_w_down)


def solution(mesh):
    return jax.shard_map(
        local,
        mesh=mesh,
        in_specs=(
            P(("node", "dev"), None),
            P(("node", "dev"), None),
            P(("node", "dev"), None),
            P(("node", "dev"), None),
            P(),
            P(None, "dev", "node"),
            P(None, "dev", "node"),
            P(None, "node", "dev"),
        ),
        out_specs=(
            P(("node", "dev"), None),
            P(("node", "dev"), None),
            P(None, "dev", "node"),
            P(None, "dev", "node"),
            P(None, "node", "dev"),
        ),
        check_vma=False,
    )
```

```python
import functools

import jax
import jax.numpy as jnp
from jax import lax
from jax.experimental import pallas as pl
from jax.experimental.pallas import tpu as pltpu
from jax.sharding import PartitionSpec as P

REPS = 2
CAP = 2
PER = REPS * CAP
F32 = jnp.float32
BF16 = jnp.bfloat16


NZ = 4
MESH = pl.DeviceIdType.MESH


def middle_kernel(
    nd, hid, pre, gate, full, from_y, stage, from_z, ys, yr, zs, zr, bs, br, fs, fr
):
    ny = nd // NZ
    me = lax.axis_index("dev")
    z = me // ny
    y = me % ny
    barrier = pltpu.get_barrier_semaphore()
    for i in range(1, ny):
        peer = z * ny + (y + i) % ny
        pl.semaphore_signal(barrier, inc=1, device_id={"dev": peer}, device_id_type=MESH)
    for k in range(1, NZ):
        peer = ((z + k) % NZ) * ny + y
        pl.semaphore_signal(barrier, inc=1, device_id={"dev": peer}, device_id_type=MESH)
    pl.semaphore_wait(barrier, ny - 1 + NZ - 1)

    def remote(src, dst, send, recv, peer):
        return pltpu.make_async_remote_copy(
            src_ref=src,
            dst_ref=dst,
            send_sem=send,
            recv_sem=recv,
            device_id={"dev": peer},
            device_id_type=MESH,
        )

    order = [k % NZ for k in range(1, NZ + 1)]
    first = {}
    for k in order:
        zk = (z + k) % NZ
        for i in range(1, ny):
            yi = (y + i) % ny
            c = remote(
                pre.at[zk * ny + yi], from_y.at[i, k], ys.at[i, k], yr.at[i, k], z * ny + yi
            )
            c.start()
            first[i, k] = c
    second = {}
    total = None
    for k in order:
        zk = (z + k) % NZ
        acc = pre[zk * ny + y].astype(F32)
        for i in range(1, ny):
            first[i, k].wait_recv()
            acc = acc + from_y[i, k].astype(F32)
        if k:
            stage[k] = acc.astype(BF16)
            c = remote(stage.at[k], from_z.at[k], zs.at[k], zr.at[k], zk * ny + y)
            c.start()
            second[k] = c
        else:
            total = acc
    for k in range(1, NZ):
        second[k].wait_recv()
        total = total + from_z[k].astype(F32)
    g, u, b = total[:, :hid], total[:, hid : 2 * hid], total[:, 2 * hid :]
    rg = gate[:, 0:1]
    sig = jax.nn.sigmoid(g)
    act = g * sig
    hidden = act * u
    scaled = rg * b
    terms = jnp.sum(b * hidden, axis=1, keepdims=True)
    t1 = terms.astype(BF16).astype(F32)
    t2 = (terms - t1).astype(BF16).astype(F32)
    t3 = terms - t1 - t2
    lane = lax.broadcasted_iota(jnp.int32, (g.shape[0], 128), 1)
    tail = jnp.where(lane == 0, t1, jnp.where(lane == 1, t2, jnp.where(lane == 2, t3, 0.0)))
    full[me, :, :hid] = (scaled * u * sig * (1.0 + g * (1.0 - sig))).astype(BF16)
    full[me, :, hid : 2 * hid] = (scaled * act).astype(BF16)
    full[me, :, 2 * hid : 3 * hid] = (rg * hidden).astype(BF16)
    full[me, :, 3 * hid :] = tail.astype(BF16)
    third = {}
    fourth = {}
    for k in range(1, NZ):
        c = remote(full.at[me], full.at[me], bs.at[k], br.at[k], ((z + k) % NZ) * ny + y)
        c.start()
        third[k] = c
    for k in range(NZ):
        src = ((z + NZ - k) % NZ) * ny + y
        if k:
            third[k].wait_recv()
        for i in range(1, ny):
            c = remote(full.at[src], full.at[src], fs.at[i, k], fr.at[i, k], z * ny + (y + i) % ny)
            c.start()
            fourth[i, k] = c
    for c in fourth.values():
        c.wait_recv()
    for group in (first, second, third, fourth):
        for c in group.values():
            c.wait_send()


def middle(pre, gate, hid):
    nd, part, wide = pre.shape
    ny = nd // NZ
    dma = pltpu.SemaphoreType.DMA
    return pl.pallas_call(
        functools.partial(middle_kernel, nd, hid),
        out_shape=jax.ShapeDtypeStruct((nd, part, wide + 128), BF16),
        in_specs=[pl.BlockSpec(memory_space=pltpu.VMEM)] * 2,
        out_specs=pl.BlockSpec(memory_space=pltpu.VMEM),
        scratch_shapes=[
            pltpu.VMEM((ny, NZ, part, wide), BF16),
            pltpu.VMEM((NZ, part, wide), BF16),
            pltpu.VMEM((NZ, part, wide), BF16),
            dma((ny, NZ)),
            dma((ny, NZ)),
            dma((NZ,)),
            dma((NZ,)),
            dma((NZ,)),
            dma((NZ,)),
            dma((ny, NZ)),
            dma((ny, NZ)),
        ],
        compiler_params=pltpu.CompilerParams(
            collective_id=0, has_side_effects=True, vmem_limit_bytes=48 * 1024 * 1024
        ),
    )(pre, gate)


def choose(expert_ids, router_gates, slot_plan, slots, experts):
    tok = expert_ids.shape[0]
    total = slot_plan.shape[0]
    live = slot_plan[:, 0] < slots
    ids = jnp.arange(total, dtype=jnp.int32)
    rank = jnp.sum(jnp.where((ids[None, :] < ids[:, None]) & live[None, :], 1, 0), axis=1)
    hot = jnp.sum(
        jnp.where(live[None, :] & (rank[None, :] == jnp.arange(experts)[:, None]), ids[None, :], 0),
        axis=1,
    )
    match = expert_ids[None, :, :] == hot[:, None, None]
    named = jnp.any(match, axis=2)
    gate = jnp.sum(jnp.where(match, router_gates.astype(F32)[None], 0.0), axis=2)
    t = jnp.arange(tok)
    before = (t[:, None] < t[None, :]).astype(BF16)
    order = jnp.dot(named.astype(BF16), before, preferred_element_type=F32)
    pick = named[:, None, :] & (order[:, None, :] == jnp.arange(PER, dtype=F32)[None, :, None])
    row_gate = jnp.sum(jnp.where(pick, gate[:, None, :], 0.0), axis=2)
    return pick.reshape(experts * PER, tok).astype(BF16), row_gate.reshape(-1), match


def local(tokens, grad_out, router_gates, expert_ids, slot_plan, w_gate, w_up, w_down):
    nd = lax.axis_size("dev")
    nn = lax.axis_size("node")
    tok, width = tokens.shape
    experts, cols, hid = w_gate.shape
    rows = experts * PER
    pick, row_gate, match = choose(expert_ids, router_gates, slot_plan, nd, experts)
    x_rows = jnp.dot(pick, tokens, preferred_element_type=F32).astype(BF16)
    dy_rows = jnp.dot(pick, grad_out, preferred_element_type=F32).astype(BF16)
    x_rows = x_rows.reshape(rows, nd, cols).transpose(1, 0, 2)
    dy_rows = dy_rows.reshape(rows, nd, cols).transpose(1, 0, 2)
    gate_cols = jnp.broadcast_to(row_gate.astype(BF16)[None, :, None], (nd, rows, 128))
    dy_rows = jnp.concatenate([dy_rows, gate_cols], axis=2)
    x_got = lax.all_to_all(x_rows, "dev", split_axis=0, concat_axis=0, tiled=True)
    x_got = lax.all_gather(x_got, "node", axis=0, tiled=False)
    dy_got = lax.all_to_all(dy_rows, "dev", split_axis=0, concat_axis=0, tiled=True)
    dy_got = lax.all_gather(dy_got, "node", axis=0, tiled=False)
    per_expert = nn * nd * PER
    xs = x_got.reshape(nn, nd, experts, PER, cols).transpose(2, 0, 1, 3, 4)
    xs = xs.reshape(experts, per_expert, cols)
    dys = dy_got[..., :cols].reshape(nn, nd, experts, PER, cols).transpose(2, 0, 1, 3, 4)
    dys = dys.reshape(experts, per_expert, cols)
    gates = dy_got[..., cols].reshape(nn, nd, experts, PER).transpose(2, 0, 1, 3)
    part = experts * per_expert // nd
    gates = gates.reshape(nd, part)
    me = lax.axis_index("dev")
    my_gate = jnp.sum(
        jnp.where(jnp.arange(nd)[:, None] == me, gates.astype(F32), 0.0), axis=0
    )[:, None]

    def widen(a, b, spec):
        r = jnp.einsum(spec, a, b, preferred_element_type=F32).astype(BF16)
        return r.reshape(nd, part, hid)

    pre = jnp.concatenate(
        [
            widen(xs, w_gate, "jrd,jdh->jrh"),
            widen(xs, w_up, "jrd,jdh->jrh"),
            widen(dys, w_down, "jrd,jhd->jrh"),
        ],
        axis=2,
    )
    full = middle(pre, jnp.broadcast_to(my_gate, (part, 128)), hid)
    full = full.reshape(experts, per_expert, -1)
    dg, du, sh = full[..., :hid], full[..., hid : 2 * hid], full[..., 2 * hid : 3 * hid]
    terms = jnp.sum(full[..., 3 * hid :].astype(F32), axis=-1, keepdims=True)
    row_grad = jnp.einsum("jrh,jdh->jrd", dg, w_gate, preferred_element_type=F32)
    row_grad = row_grad + jnp.einsum("jrh,jdh->jrd", du, w_up, preferred_element_type=F32)
    row_grad = jnp.concatenate(
        [row_grad, jnp.broadcast_to(terms, terms.shape[:2] + (128,))], axis=2
    )
    row_grad = row_grad.reshape(experts, nn, nd, PER, cols + 128).transpose(1, 2, 0, 3, 4)
    row_grad = row_grad.reshape(nn, nd, rows, cols + 128)
    row_grad = lax.all_to_all(row_grad, "node", split_axis=0, concat_axis=0, tiled=True)
    row_grad = jnp.sum(row_grad, axis=0)
    back_rows = lax.all_to_all(row_grad, "dev", split_axis=0, concat_axis=0, tiled=True)
    mine = back_rows[0, :, cols].reshape(experts, PER, 1)
    back_rows = back_rows[:, :, :cols].transpose(1, 0, 2).reshape(rows, width)
    high = back_rows.astype(BF16)
    low = (back_rows - high.astype(F32)).astype(BF16)
    grad_tokens = jnp.einsum(
        "qt,qd->td",
        jnp.concatenate([pick, pick], axis=0),
        jnp.concatenate([high, low], axis=0),
        preferred_element_type=F32,
    ).astype(BF16)
    pair_val = jnp.sum(jnp.where(pick.reshape(experts, PER, tok) > 0, mine, 0.0), axis=1)
    grad_gates = jnp.sum(jnp.where(match, pair_val[:, :, None], 0.0), axis=0)
    grad_w_gate = jnp.einsum("jrd,jrh->jdh", xs, dg, preferred_element_type=F32).astype(BF16)
    grad_w_up = jnp.einsum("jrd,jrh->jdh", xs, du, preferred_element_type=F32).astype(BF16)
    grad_w_down = jnp.einsum("jrh,jrd->jhd", sh, dys, preferred_element_type=F32).astype(BF16)
    return (grad_tokens, grad_gates, grad_w_gate, grad_w_up, grad_w_down)


def solution(mesh):
    return jax.shard_map(
        local,
        mesh=mesh,
        in_specs=(
            P(("node", "dev"), None),
            P(("node", "dev"), None),
            P(("node", "dev"), None),
            P(("node", "dev"), None),
            P(),
            P(None, "dev", "node"),
            P(None, "dev", "node"),
            P(None, "node", "dev"),
        ),
        out_specs=(
            P(("node", "dev"), None),
            P(("node", "dev"), None),
            P(None, "dev", "node"),
            P(None, "dev", "node"),
            P(None, "node", "dev"),
        ),
        check_vma=False,
    )
```
